32 devices in a mesh: seq: 8 (over z, x), exp: 4 (over y, core).
Axes of the slice: x: 2, y: 2, z: 4, core: 2. Of those that a mesh axis runs over, the one named last changes fastest.
Arguments:
- tokens: bfloat16 [4096, 1536], P(('seq', 'exp')), may hold values from -6 to 6
- in_gain: float32 [1536], replicated, may hold values from 0.5 to 1.5
- in_z: bfloat16 [1536, 3072], P(None, 'exp'), may hold values from -0.15625 to 0.15625
- in_x: bfloat16 [1536, 3072], P(None, 'exp'), may hold values from -0.15625 to 0.15625
- in_bc: bfloat16 [1536, 256], replicated, may hold values from -0.15625 to 0.15625
- in_dt: bfloat16 [1536, 48], P(None, 'exp'), may hold values from -0.0390625 to 0.0390625
- conv_x: float32 [4, 3072], P(None, 'exp'), may hold values from -3 to 3
- conv_bc: float32 [4, 256], replicated, may hold values from -3 to 3
- dt_bias: float32 [48], P('exp'), may hold values from -7 to -2
- a_log: float32 [48], P('exp'), may hold values from -1 to 2.5
- d_skip: float32 [48], P('exp'), may hold values from 0.5 to 1.5
- norm_gain: float32 [3072], P('exp'), may hold values from 0.5 to 1.5
- out_w: bfloat16 [3072, 1536], P('exp'), may hold values from -0.109375 to 0.109375
- post_gain: float32 [1536], replicated, may hold values from 0.5 to 1.5
- sh_gate: bfloat16 [1536, 1024], P(None, 'exp'), may hold values from -0.15625 to 0.15625
- sh_up: bfloat16 [1536, 1024], P(None, 'exp'), may hold values from -0.15625 to 0.15625
- sh_down: bfloat16 [1024, 1536], P('exp'), may hold values from -0.1875 to 0.1875
- ex_gate: bfloat16 [32, 1536, 512], P('seq'), may hold values from -0.15625 to 0.15625
- ex_up: bfloat16 [32, 1536, 512], P('seq'), may hold values from -0.15625 to 0.15625
- ex_down: bfloat16 [32, 512, 1536], P('seq'), may hold values from -0.25 to 0.25
- routes: int32 [4096, 6], P(('seq', 'exp')), may hold values from 0 to 31, all different within a row; in each aligned block of 128 rows (0 to 127, 128 to 255, ...) at most 32 rows name the same one
- gates: float32 [4096, 6], P(('seq', 'exp')), may hold values from 0.1 to 1
- lengths: int32 [8], replicated, may hold values from 1 to 1024, 4096 in all
- cache_slot: int32 [8], replicated, may hold values from 0 to 7, each once
Outputs:
- layer_out: bfloat16 [4096, 1536], P(('seq', 'exp'))
- state_cache: float32 [8, 48, 64, 128], P('seq', 'exp')
The draws below stay inside these ranges and needn't reach their ends.
Inputs may be any that keep to these rules, and one draw needn't show every extreme that they name: `routes`: in the rows of one device (aligned blocks of 128 rows) no expert is named by more than 32 rows, a bound that some block reaches; each row names 6 different experts. The lengths sum to 4096; the largest is exactly 1024. `cache_slot`: every slot is named once.
All inputs are finite; a program needn't handle non-finite values.
Results may differ from the reference program's by a relative error of at most 0.019.
Values may be sent and summed in bfloat16 or wider, within the bound.
A program may use at most 128 MiB of HBM per device.

```python
import math
import jax
import jax.numpy as jnp
import numpy as np
from jax import lax

D = 1536
HEADS = 48
HDIM = 64
DSTATE = 128
CONV = 4
FFE = 512
FFS = 1024
TOP = 6
BLOCK = 512
TOK_DEV = 128
EXPERTS = 32
TOKENS = 4096
NREQ = 8
LONGEST = 1024
CAP = 32
DI = 3072
N_SEQ = 8
N_EXP = 4


def block_levels(rng, extent, split, low, high):
    loudness = 1.0
    for position, blocks in split:
        draws = jax.random.uniform(jax.random.fold_in(jax.random.fold_in(rng, 6), position), (blocks,), jnp.float32, low / len(split), high / len(split))
        loudness = loudness * jnp.repeat(jnp.exp(draws), extent[position] // blocks).reshape((-1,) + (1,) * (len(extent) - 1 - position))
    return loudness


def profile(amount, total, limit, lean):
    portions = [(1 << 20) // math.isqrt(standing ** lean) + 1 for standing in range(2, amount + 1)]
    surplus, given = total - limit - (amount - 1), [1] * (amount - 1)
    while surplus > 0:
        free = [i for i in range(amount - 1) if given[i] < limit]
        mass, remaining = sum([portions[i] for i in free]), surplus
        for i in free:
            addition = min(limit - given[i], max(1, remaining * portions[i] // mass), surplus)
            given[i] = given[i] + addition
            surplus = surplus - addition
    return np.array([limit] + given)


def ragged(key, count, total, most, lean):
    if count == 2:
        one = jax.random.randint(key, (), max(1, total - most), min(most, total - 1) + 1)
        return jnp.stack([one, total - one])
    sizes = jnp.asarray(profile(count, total, most, lean), jnp.int32)
    twos = (count - 1) // 2
    donor, taker = sizes[1:1 + 2 * twos:2], sizes[2:2 + 2 * twos:2]
    room = jnp.minimum(donor - 1, most - taker)
    moved = jax.random.randint(jax.random.fold_in(key, 1), (twos,), 0, 1 << 20) % (room + 1)
    sizes = sizes.at[1:1 + 2 * twos:2].set(donor - moved).at[2:2 + 2 * twos:2].set(taker + moved)
    return sizes[jax.random.permutation(jax.random.fold_in(key, 2), count)]


def deal_out(key, own, number, rows, amount, top, bound, slope):
    order = jax.random.permutation(key, amount)
    packed, ordinary = shares(amount, rows * top, bound, slope, True), shares(amount, rows * top, bound, slope, False)
    places = jnp.arange(amount)

    def named(sizes, rotation):
        used = int((sizes > 0).sum())
        fixed = max(1, used // 4)
        moved = fixed + (places - fixed + rotation * (used - fixed)) % max(1, amount - fixed)
        return jnp.zeros((amount,), jnp.int32).at[order[jnp.where(places < fixed, places, moved)]].set(jnp.asarray(sizes, jnp.int32))

    sizes = jnp.where(number % 4 == 0, named(packed, number // 4), named(ordinary, number - number // 4 - 1))
    mixed = jax.random.permutation(jax.random.fold_in(own, 3), amount)
    donor, receiver = mixed[0:amount // 2 * 2:2], mixed[1:amount // 2 * 2:2]
    margin = jnp.minimum(sizes[donor] - 1, bound - sizes[receiver]) // 2
    margin = jnp.where((donor == order[0]) | (receiver == order[0]) | (sizes[receiver] == 0), 0, jnp.maximum(margin, 0))
    moved = jax.random.randint(jax.random.fold_in(own, 4), (amount // 2,), 0, 1 << 20) % (margin + 1)
    sizes = sizes.at[donor].add(-moved).at[receiver].add(moved)
    labels = jnp.searchsorted(jnp.cumsum(sizes), jnp.arange(rows * top), side="right").astype(jnp.int32)
    listing = labels.reshape(top, rows).T
    listing = listing[jax.random.permutation(jax.random.fold_in(own, 1), rows)]
    rotation = jax.random.randint(jax.random.fold_in(own, 2), (rows, 1), 0, top)
    return jnp.take_along_axis(listing, (jnp.arange(top)[None, :] + rotation) % top, axis=1)


def shares(count, total, bound, lean, full):
    weights = [(1 << 20) // math.isqrt(grade ** lean) + 1 for grade in range(1, count + 1)]
    largest = bound if full else min(bound, max(-(-total // count), total * weights[0] // sum(weights)))
    least = 1 if total - largest >= count - 1 else 0
    holding, surplus = [largest] + [least] * (count - 1), total - largest - least * (count - 1)
    while surplus > 0:
        candidates = [i for i in range(1, count) if holding[i] < largest] or [i for i in range(1, count) if holding[i] < bound]
        whole, budget = sum([weights[i] for i in candidates]), surplus
        for i in candidates:
            addition = min(bound - holding[i], max(1, budget * weights[i] // whole), surplus)
            holding[i] = holding[i] + addition
            surplus = surplus - addition
    return np.array(holding)


def normal_values(key, shape, deviation, most, shards=(), kind=jnp.bfloat16):
    level = block_levels(key, shape, shards, -0.22, 0.18) if shards else 1.0
    values = jax.random.normal(key, shape, jnp.float32) * deviation * level
    return jnp.minimum(jnp.maximum(values, -most), most).astype(kind)


def setup_inputs(seed: int = 0) -> dict:
    splits = jax.random.split(jax.random.key(seed), 25)
    tokens = normal_values(splits[0], (TOKENS, D), 1.0, 6.0, ((0, 32),))
    in_gain = jnp.clip(1.0 + 0.1 * jax.random.normal(splits[1], (D,), jnp.float32), 0.5, 1.5)
    in_z = normal_values(splits[2], (D, DI), D ** -0.5, 0.15625, ((1, 4),))
    in_x = normal_values(splits[3], (D, DI), D ** -0.5, 0.15625, ((1, 4),))
    in_bc = normal_values(splits[4], (D, 2 * DSTATE), D ** -0.5, 0.15625)
    in_dt = normal_values(splits[5], (D, HEADS), (16 * D) ** -0.5, 0.0390625, ((1, 4),))
    conv_x = normal_values(splits[6], (CONV, DI), 0.5, 3.0, ((1, 4),), jnp.float32)
    conv_bc = normal_values(splits[7], (CONV, 2 * DSTATE), 0.5, 3.0, (), jnp.float32)
    dt_bias = jnp.clip(-7.0 + 5.0 * jax.random.uniform(splits[8], (HEADS,), jnp.float32) ** block_levels(splits[8], (HEADS,), ((0, 4),), -0.2, 0.2), -7.0, -2.0)
    a_log = jnp.clip(-1.0 + 3.5 * jax.random.uniform(splits[9], (HEADS,), jnp.float32) ** block_levels(splits[9], (HEADS,), ((0, 4),), -0.2, 0.2), -1.0, 2.5)
    d_skip = jnp.clip(0.5 + 1.0 * jax.random.uniform(splits[10], (HEADS,), jnp.float32) ** block_levels(splits[10], (HEADS,), ((0, 4),), -0.2, 0.2), 0.5, 1.5)
    norm_gain = jnp.clip(1.0 + 0.1 * jax.random.normal(splits[11], (DI,), jnp.float32), 0.5, 1.5)
    out_w = normal_values(splits[12], (DI, D), DI ** -0.5, 0.109375, ((0, 4),))
    post_gain = jnp.clip(1.0 + 0.1 * jax.random.normal(splits[13], (D,), jnp.float32), 0.5, 1.5)
    sh_gate = normal_values(splits[14], (D, FFS), D ** -0.5, 0.15625, ((1, 4),))
    sh_up = normal_values(splits[15], (D, FFS), D ** -0.5, 0.15625, ((1, 4),))
    sh_down = normal_values(splits[16], (FFS, D), FFS ** -0.5, 0.1875, ((0, 4),))
    ex_gate = normal_values(splits[17], (EXPERTS, D, FFE), D ** -0.5, 0.15625, ((0, 8),))
    ex_up = normal_values(splits[18], (EXPERTS, D, FFE), D ** -0.5, 0.15625, ((0, 8),))
    ex_down = normal_values(splits[19], (EXPERTS, FFE, D), FFE ** -0.5, 0.25, ((0, 8),))
    routes_keys = jax.random.split(jax.random.fold_in(splits[20], 1), TOKENS // TOK_DEV)
    routes_turns = jax.random.permutation(jax.random.fold_in(splits[20], 3), TOKENS // TOK_DEV)
    routes = jax.vmap(lambda own, number: deal_out(jax.random.fold_in(splits[20], 2), own, number, TOK_DEV, EXPERTS, TOP, CAP, 1))(routes_keys, routes_turns).reshape((TOKENS, TOP))
    gates = jnp.clip(0.1 + 0.9 * jax.random.uniform(splits[21], (TOKENS, TOP), jnp.float32) ** block_levels(splits[21], (TOKENS, TOP), ((0, 32),), -0.2, 0.2), 0.1, 1.0)
    lengths = ragged(splits[22], NREQ, TOKENS, LONGEST, 2).astype(jnp.int32)
    cache_slot = jax.random.permutation(splits[23], NREQ).astype(jnp.int32)
    return dict(tokens=tokens, in_gain=in_gain, in_z=in_z, in_x=in_x, in_bc=in_bc, in_dt=in_dt, conv_x=conv_x, conv_bc=conv_bc, dt_bias=dt_bias, a_log=a_log, d_skip=d_skip, norm_gain=norm_gain, out_w=out_w, post_gain=post_gain, sh_gate=sh_gate, sh_up=sh_up, sh_down=sh_down, ex_gate=ex_gate, ex_up=ex_up, ex_down=ex_down, routes=routes, gates=gates, lengths=lengths, cache_slot=cache_slot)


epsilon = 1e-05
highest = lax.Precision.HIGHEST

def rms_rows(values, gain):
    meansq = lax.optimization_barrier(jnp.mean(values * values, axis=-1, keepdims=True))
    return values * lax.rsqrt(meansq + epsilon) * gain

def segment_of(positions, req_ends):
    return lax.optimization_barrier(jnp.sum((positions[:, None] >= req_ends[None, :]).astype(jnp.int32), axis=1)).astype(jnp.int32)

def causal_conv(inputs, weight, segment):
    total = inputs.shape[0]
    summed = jnp.zeros(inputs.shape, jnp.float32)
    for tap in range(CONV):
        lag = CONV - 1 - tap
        shifted = jnp.pad(inputs.astype(jnp.float32), ((lag, 0), (0, 0)))[:total]
        earlier = jnp.pad(segment, (lag, 0), constant_values=-1)[:total]
        kept = (earlier == segment)[:, None]
        summed = summed + jnp.where(kept, weight[tap] * shifted, 0.0)
    return jax.nn.silu(summed).astype(jnp.bfloat16)

def block_step(state, block):
    drive_x, b_rows, c_rows, log_decay, step_size, segment, before_seg = block
    length = segment.shape[0]
    cumulative = jnp.cumsum(log_decay, axis=0)
    order = jnp.arange(length, dtype=jnp.int32)
    same = (segment[:, None] == segment[None, :]) & (order[:, None] >= order[None, :])
    log_gap = cumulative[:, None, :] - cumulative[None, :, :]
    decay = jnp.where(same[:, :, None], jnp.exp(jnp.where(same[:, :, None], log_gap, 0.0)), 0.0)
    scores = jnp.dot(c_rows, b_rows.T, preferred_element_type=jnp.float32)
    drive = drive_x.astype(jnp.float32) * step_size[:, :, None]
    weights = scores[:, :, None] * decay
    outputs = jnp.einsum('tsh,shp->thp', weights, drive, precision=highest)
    c_float = c_rows.astype(jnp.float32)
    b_float = b_rows.astype(jnp.float32)
    entry = jnp.where((segment == before_seg)[:, None], jnp.exp(cumulative), 0.0)
    outputs = outputs + entry[:, :, None] * jnp.einsum('tn,hpn->thp', c_float, state, precision=highest)
    last_seg = segment[length - 1]
    tail = jnp.where((segment == last_seg)[:, None], jnp.exp(cumulative[length - 1][None, :] - cumulative), 0.0)
    persist = jnp.where(last_seg == before_seg, jnp.exp(cumulative[length - 1]), 0.0)
    new_state = persist[:, None, None] * state + jnp.einsum('sh,shp,sn->hpn', tail, drive, b_float, precision=highest)
    return (new_state, outputs)

def reference(tokens, in_gain, in_z, in_x, in_bc, in_dt, conv_x, conv_bc, dt_bias, a_log, d_skip, norm_gain, out_w, post_gain, sh_gate, sh_up, sh_down, ex_gate, ex_up, ex_down, routes, gates, lengths, cache_slot):
    total = tokens.shape[0]
    normed_in = rms_rows(tokens.astype(jnp.float32), in_gain).astype(jnp.bfloat16)
    gate_raw = jnp.dot(normed_in, in_z, preferred_element_type=jnp.float32).astype(jnp.bfloat16)
    conv_in_x = jnp.dot(normed_in, in_x, preferred_element_type=jnp.float32).astype(jnp.bfloat16)
    conv_in_bc = jnp.dot(normed_in, in_bc, preferred_element_type=jnp.float32).astype(jnp.bfloat16)
    dt_raw = jnp.dot(normed_in, in_dt, preferred_element_type=jnp.float32).astype(jnp.bfloat16)
    req_ends = jnp.cumsum(lengths).astype(jnp.int32)
    positions = jnp.arange(total, dtype=jnp.int32)
    segment = segment_of(positions, req_ends)
    conv_x_out = causal_conv(conv_in_x, conv_x, segment)
    conv_bc_out = causal_conv(conv_in_bc, conv_bc, segment)
    b_all = conv_bc_out[:, :DSTATE]
    c_all = conv_bc_out[:, DSTATE:]
    step_size = jax.nn.softplus(dt_raw.astype(jnp.float32) + dt_bias)
    log_decay = -step_size * jnp.exp(a_log)
    heads_x = conv_x_out.reshape(total, HEADS, HDIM)
    before_all = jnp.concatenate([jnp.full((1,), -1, jnp.int32), segment[:-1]])
    count = total // BLOCK

    def blocked(values):
        return values.reshape((count, BLOCK) + values.shape[1:])
    blocks = (blocked(heads_x), blocked(b_all), blocked(c_all), blocked(log_decay), blocked(step_size), blocked(segment), blocked(before_all)[:, 0])
    start_state = jnp.zeros((HEADS, HDIM, DSTATE), jnp.float32)
    final_state, outputs = lax.scan(block_step, start_state, blocks)
    mixed_y = outputs.reshape(total, HEADS, HDIM) + d_skip[None, :, None] * heads_x.astype(jnp.float32)
    gated = mixed_y.reshape(total, DI) * jax.nn.silu(gate_raw.astype(jnp.float32))
    meansq = lax.optimization_barrier(jnp.sum(gated * gated, axis=1)) / DI
    scaled = (gated * lax.rsqrt(meansq + epsilon)[:, None] * norm_gain).astype(jnp.bfloat16)
    group_width = DI // N_EXP
    mixer_out = jnp.zeros((total, D), jnp.float32)
    for group_idx in range(N_EXP):
        lo_col = group_idx * group_width
        term = jnp.dot(scaled[:, lo_col:lo_col + group_width], out_w[lo_col:lo_col + group_width], preferred_element_type=jnp.float32)
        mixer_out = mixer_out + lax.optimization_barrier(term.astype(jnp.bfloat16)).astype(jnp.float32)
    residual = tokens.astype(jnp.float32) + mixer_out
    normed = rms_rows(residual, post_gain).astype(jnp.bfloat16)
    shared_hidden = (jax.nn.silu(jnp.dot(normed, sh_gate, preferred_element_type=jnp.float32)) * jnp.dot(normed, sh_up, preferred_element_type=jnp.float32)).astype(jnp.bfloat16)
    shared_width = FFS // N_EXP
    shared = jnp.zeros((total, D), jnp.float32)
    for group_idx in range(N_EXP):
        lo_col = group_idx * shared_width
        term = jnp.dot(shared_hidden[:, lo_col:lo_col + shared_width], sh_down[lo_col:lo_col + shared_width], preferred_element_type=jnp.float32)
        shared = shared + lax.optimization_barrier(term.astype(jnp.bfloat16)).astype(jnp.float32)
    flat_routes = routes.reshape(-1)
    flat_gates = gates.reshape(-1)
    most_rows = CAP * N_SEQ * N_EXP

    def expert_pass(routed, item):
        gate_e, up_e, down_e, expert_id = item
        chosen = flat_routes == expert_id
        found = jnp.nonzero(chosen, size=most_rows, fill_value=0)[0].astype(jnp.int32)
        valid = jnp.arange(most_rows, dtype=jnp.int32) < jnp.sum(chosen.astype(jnp.int32)).astype(jnp.int32)
        token_idx = found // TOP
        rows_in = normed[token_idx]
        hidden = (jax.nn.silu(jnp.dot(rows_in, gate_e, preferred_element_type=jnp.float32)) * jnp.dot(rows_in, up_e, preferred_element_type=jnp.float32)).astype(jnp.bfloat16)
        result = jnp.dot(hidden, down_e, preferred_element_type=jnp.float32).astype(jnp.bfloat16)
        weight_rows = jnp.where(valid, flat_gates[found], 0.0)
        routed = routed.at[token_idx].add(weight_rows[:, None] * result.astype(jnp.float32))
        return (routed, None)
    routed, _ = lax.scan(expert_pass, jnp.zeros((total, D), jnp.float32), (ex_gate, ex_up, ex_down, jnp.arange(ex_gate.shape[0], dtype=jnp.int32)))
    layer_out = (residual + shared + routed).astype(jnp.bfloat16)
    req_starts = (req_ends - lengths).astype(jnp.int32)
    pad_x = jnp.concatenate([heads_x.astype(jnp.float32) * step_size[:, :, None], jnp.zeros((LONGEST, HEADS, HDIM), jnp.float32)])
    pad_b = jnp.concatenate([b_all.astype(jnp.float32), jnp.zeros((LONGEST, DSTATE), jnp.float32)])
    pad_decay = jnp.concatenate([log_decay, jnp.zeros((LONGEST, HEADS), jnp.float32)])

    def request_state(req_idx):
        start = req_starts[req_idx]
        kept = jnp.arange(LONGEST, dtype=jnp.int32) < lengths[req_idx]
        drive = lax.dynamic_slice_in_dim(pad_x, start, LONGEST, 0)
        b_rows = lax.dynamic_slice_in_dim(pad_b, start, LONGEST, 0)
        decay_rows = jnp.where(kept[:, None], lax.dynamic_slice_in_dim(pad_decay, start, LONGEST, 0), 0.0)
        suffix = jnp.cumsum(decay_rows[::-1], axis=0)[::-1]
        after = jnp.concatenate([suffix[1:], jnp.zeros((1, HEADS), jnp.float32)])
        weights = jnp.where(kept[:, None], jnp.exp(after), 0.0)
        return jnp.einsum('sh,shp,sn->hpn', weights, drive, b_rows, precision=highest)
    states = lax.map(request_state, jnp.arange(NREQ, dtype=jnp.int32))
    state_cache = jnp.zeros((NREQ, HEADS, HDIM, DSTATE), jnp.float32).at[cache_slot].set(states)
    return (layer_out, state_cache)
```

```python
import functools
import jax
import jax.numpy as jnp
from jax import lax
from jax.experimental import pallas as pl
from jax.experimental.pallas import tpu as pltpu
from jax.sharding import PartitionSpec as P

DI = 3072


epsilon = 1e-05
highest = lax.Precision.HIGHEST


def from_behind(block, axis, distance):
    devices = range(lax.axis_size(axis))
    route = [(i - distance, i) for i in devices if i - distance in devices]
    return lax.ppermute(block, axis, route)


def rms_rows(values, gain):
    meansq = jnp.mean(values * values, axis=-1, keepdims=True)
    return values * lax.rsqrt(meansq + epsilon) * gain


LANES = 128
HALF = 64


def call(kernel, outs, scratch, flops, *operands):
    moved = sum(v.size * v.dtype.itemsize for v in operands)
    smem = [v.dtype == jnp.int32 and v.ndim == 1 for v in operands]
    return pl.pallas_call(
        kernel,
        out_shape=[jax.ShapeDtypeStruct(s, t) for s, t in outs],
        in_specs=[pl.BlockSpec(memory_space=pltpu.SMEM if m else pltpu.VMEM) for m in smem],
        out_specs=[pl.BlockSpec(memory_space=pltpu.VMEM) for _ in outs],
        scratch_shapes=scratch,
        compiler_params=pltpu.CompilerParams(vmem_limit_bytes=48 * 1024 * 1024),
        cost_estimate=pl.CostEstimate(flops=int(flops), bytes_accessed=moved, transcendentals=0),
    )(*operands)


def positions(shape, axis, start, lag=0):
    return lax.broadcasted_iota(jnp.int32, shape, axis) + (start - lag)


def segments(pos, meta, req_count):
    seg = jnp.zeros(pos.shape, jnp.int32)
    for req in range(req_count):
        seg = seg + (pos >= meta[1 + req]).astype(jnp.int32)
    return seg


def scalar_segment(pos, meta, req_count):
    seg = jnp.int32(0)
    for req in range(req_count):
        seg = seg + (pos >= meta[1 + req]).astype(jnp.int32)
    return seg


def before_segment(meta, req_count):
    start = meta[0]
    return jnp.where(start > 0, scalar_segment(start - 1, meta, req_count), -1)


def by_head(values, pair):
    rows = values.shape[0]
    lane = lax.broadcasted_iota(jnp.int32, (rows, LANES), 1)
    return jnp.where(lane < HALF, values[:, 2 * pair : 2 * pair + 1], values[:, 2 * pair + 1 : 2 * pair + 2])


def front_kernel(
    req_count, heads, meta, xin, bcin, dt_raw, edge, conv_x, conv_bc, dt_bias, a_log,
    xc, bc, drive, drive_wt, cum, cum_t, lead, packet, ext,
):
    rows, channels = xin.shape
    start = meta[0]
    ext[0:8, :] = edge[8:16, :].astype(jnp.float32)
    ext[8:, :channels] = xin[...].astype(jnp.float32)
    ext[8:, channels:] = bcin[...].astype(jnp.float32)
    shape = (rows, LANES)
    seg = segments(positions(shape, 0, start), meta, req_count)
    kept = []
    for lag in (3, 2, 1):
        pos = positions(shape, 0, start, lag)
        kept.append((segments(pos, meta, req_count) == seg) & (pos >= 0))
    kept.append(None)

    def conv(column, weight, offset):
        total = jnp.zeros(shape, jnp.float32)
        for tap in range(4):
            window = ext[5 + tap : 5 + tap + rows, column : column + LANES]
            term = weight[tap : tap + 1, offset : offset + LANES] * window
            total = total + (term if kept[tap] is None else jnp.where(kept[tap], term, 0.0))
        return (total * jax.nn.sigmoid(total)).astype(jnp.bfloat16)

    for part in range(2):
        bc[:, part * LANES : (part + 1) * LANES] = conv(channels + part * LANES, conv_bc, part * LANES)
    raw = dt_raw[...].astype(jnp.float32) + dt_bias[...]
    step = jnp.maximum(raw, 0.0) + jnp.log1p(jnp.exp(-jnp.abs(raw)))
    log_decay = -step * jnp.exp(a_log[...])
    lower = (
        lax.broadcasted_iota(jnp.int32, (rows, rows), 0)
        >= lax.broadcasted_iota(jnp.int32, (rows, rows), 1)
    ).astype(jnp.float32)
    total = jnp.dot(lower, log_decay, precision=highest, preferred_element_type=jnp.float32)
    cum[...] = total
    cum_t[...] = total.T
    seg_before = before_segment(meta, req_count)
    lead[...] = jnp.where(seg == seg_before, jnp.exp(total), 0.0)
    seg_end = total
    for req in range(req_count):
        row = jnp.clip(meta[1 + req] - 1 - start, 0, rows - 1)
        seg_end = jnp.where(seg == req, cum[pl.ds(row, 1), :], seg_end)
    weight = step * jnp.exp(jnp.minimum(seg_end - total, 0.0))
    seg_last = scalar_segment(start + rows - 1, meta, req_count)
    b_last = jnp.where(seg == seg_last, bc[:, :LANES].astype(jnp.float32), 0.0).astype(jnp.bfloat16)
    for pair in range(heads // 2):
        cols = slice(pair * LANES, (pair + 1) * LANES)
        values = conv(pair * LANES, conv_x, pair * LANES)
        xc[:, cols] = values
        wide = values.astype(jnp.float32)
        drive[:, cols] = (wide * by_head(step, pair)).astype(jnp.bfloat16)
        turned = (wide * by_head(weight, pair)).T.astype(jnp.bfloat16)
        drive_wt[cols, :] = turned
        packet[cols, :] = jnp.dot(turned, b_last, preferred_element_type=jnp.float32).astype(jnp.bfloat16)
    passing = jnp.where(seg_last == seg_before, jnp.exp(total[rows - 1 : rows, :]), 0.0)
    high = passing.astype(jnp.bfloat16).astype(jnp.float32)
    row = lax.broadcasted_iota(jnp.int32, (16, LANES), 0)
    packet[channels:, :] = jnp.where(row == 0, high, jnp.where(row == 1, passing - high, 0.0)).astype(jnp.bfloat16)


def local_kernel(req_count, heads, meta, bc, xc, drive, cum, cum_t, d_skip, mixed):
    rows = xc.shape[0]
    start = meta[0]
    tile = LANES
    lane = lax.broadcasted_iota(jnp.int32, (tile, LANES), 1)
    for i in range(rows // tile):
        at = slice(i * tile, (i + 1) * tile)
        width = (i + 1) * tile
        pos_t = positions((tile, width), 0, start + i * tile)
        pos_s = positions((tile, width), 1, start)
        seg_t = segments(positions((tile, LANES), 0, start + i * tile), meta, req_count)[:, 0:1]
        seg_s = segments(positions((8, width), 1, start), meta, req_count)[0:1, :]
        scores = lax.dot_general(
            bc[at, LANES:], bc[0:width, :LANES], (((1,), (1,)), ((), ())), preferred_element_type=jnp.float32
        )
        scores = jnp.where((seg_t == seg_s) & (pos_t >= pos_s), scores, 0.0)
        for pair in range(heads // 2):
            cols = slice(pair * LANES, (pair + 1) * LANES)
            parts = []
            for head in (2 * pair, 2 * pair + 1):
                gap = cum[at, head : head + 1] - cum_t[head : head + 1, 0:width]
                decayed = (scores * jnp.exp(jnp.minimum(gap, 0.0))).astype(jnp.bfloat16)
                parts.append(jnp.dot(decayed, drive[0:width, cols], preferred_element_type=jnp.float32))
            skip = by_head(d_skip[...], pair) * xc[at, cols].astype(jnp.float32)
            mixed[at, cols] = jnp.where(lane < HALF, parts[0], parts[1]) + skip


def cache_kernel(req_count, heads, meta, bc, drive_wt, cum, packets, state_in, placed):
    channels, rows = drive_wt.shape
    start = meta[0]
    hops = packets.shape[0]
    for head in range(heads):
        at = slice(head * HALF, (head + 1) * HALF)
        state = packets[hops - 1, at, :].astype(jnp.float32)
        for hop in range(hops - 2, -1, -1):
            passing = packets[hop, channels : channels + 16, head : head + 1].astype(jnp.float32)
            scale = passing[0:1] + passing[1:2]
            state = scale * state + packets[hop, at, :].astype(jnp.float32)
        state_in[at, :] = state.astype(jnp.bfloat16)
    seg = segments(positions((rows, LANES), 0, start), meta, req_count)
    seg_before = before_segment(meta, req_count)
    for req in range(req_count):
        slot = meta[1 + req_count + req]
        end = meta[1 + req] - 1 - start
        inside = (end >= 0) & (end < rows)

        @pl.when(inside)
        def _():
            b_own = jnp.where(seg == req, bc[:, :LANES].astype(jnp.float32), 0.0).astype(jnp.bfloat16)
            last = cum[pl.ds(jnp.clip(end, 0, rows - 1), 1), :]
            holding = jnp.where(seg_before == req, jnp.exp(last), 0.0)
            fresh = jnp.dot(drive_wt[...], b_own, preferred_element_type=jnp.float32)
            for head in range(heads):
                at = slice(head * HALF, (head + 1) * HALF)
                held = holding[:, head : head + 1] * state_in[at, :].astype(jnp.float32)
                placed[slot, at, :] = (fresh[at] + held).astype(jnp.bfloat16)

        @pl.when(jnp.logical_not(inside))
        def _():
            placed[slot] = jnp.zeros((channels, LANES), jnp.bfloat16)


def gate_kernel(heads, mixed, gate_raw, bc, state_in, lead, gain, gated, square):
    rows = mixed.shape[0]
    total = jnp.zeros((rows, LANES), jnp.float32)
    for pair in range(heads // 2):
        cols = slice(pair * LANES, (pair + 1) * LANES)
        carried = lax.dot_general(
            bc[:, LANES:], state_in[cols, :], (((1,), (1,)), ((), ())), preferred_element_type=jnp.float32
        )
        raw = gate_raw[:, cols].astype(jnp.float32)
        value = (mixed[:, cols] + by_head(lead[...], pair) * carried) * (raw * jax.nn.sigmoid(raw))
        total = total + value * value
        gated[:, cols] = (value * gain[:, cols]).astype(jnp.bfloat16)
    square[...] = jnp.broadcast_to(jnp.sum(total, axis=1, keepdims=True), (rows, LANES))


def body(
    tokens,
    in_gain,
    in_z,
    in_x,
    in_bc,
    in_dt,
    conv_x,
    conv_bc,
    dt_bias,
    a_log,
    d_skip,
    norm_gain,
    out_w,
    post_gain,
    sh_gate,
    sh_up,
    sh_down,
    ex_gate,
    ex_up,
    ex_down,
    routes,
    gates,
    lengths,
    cache_slot,
):
    seq_count = lax.axis_size("seq")
    own_rows = tokens.shape[0]
    width = tokens.shape[1]
    state_size = in_bc.shape[1] // 2
    local_heads = a_log.shape[0]
    head_width = conv_x.shape[1] // local_heads
    stream = lax.all_gather(tokens, "exp", axis=0, tiled=True)
    row_count = stream.shape[0]
    normed_in = rms_rows(stream.astype(jnp.float32), in_gain).astype(jnp.bfloat16)
    conv_in_x = jnp.dot(normed_in, in_x, preferred_element_type=jnp.float32).astype(jnp.bfloat16)
    conv_in_bc = jnp.dot(normed_in, in_bc, preferred_element_type=jnp.float32).astype(jnp.bfloat16)
    dt_raw = jnp.dot(normed_in, jnp.pad(in_dt, ((0, 0), (0, LANES - local_heads))), preferred_element_type=jnp.float32).astype(jnp.bfloat16)
    tail_rows = jnp.concatenate([conv_in_x[row_count - 16 :], conv_in_bc[row_count - 16 :]], axis=1)
    edge_rows = from_behind(tail_rows, "seq", 1)
    gate_raw = jnp.dot(normed_in, in_z, preferred_element_type=jnp.float32).astype(jnp.bfloat16)
    req_ends = jnp.cumsum(lengths)
    stream_start = lax.axis_index("seq") * row_count
    meta = jnp.concatenate([jnp.reshape(stream_start, (1,)), req_ends, cache_slot]).astype(jnp.int32)
    channels = conv_in_x.shape[1]

    def lanes(values):
        return jnp.pad(values, (0, LANES - values.shape[0]))[None]

    xc, bc, drive, drive_wt, cum, cum_t, lead, packet = call(
        functools.partial(front_kernel, lengths.shape[0], local_heads),
        [
            ((row_count, channels), jnp.bfloat16),
            ((row_count, 2 * state_size), jnp.bfloat16),
            ((row_count, channels), jnp.bfloat16),
            ((channels, row_count), jnp.bfloat16),
            ((row_count, LANES), jnp.float32),
            ((LANES, row_count), jnp.float32),
            ((row_count, LANES), jnp.float32),
            ((channels + 16, state_size), jnp.bfloat16),
        ],
        [pltpu.VMEM((row_count + 8, channels + 2 * state_size), jnp.float32)],
        3e8,
        meta,
        conv_in_x,
        conv_in_bc,
        dt_raw,
        edge_rows,
        conv_x,
        conv_bc,
        lanes(dt_bias),
        lanes(a_log),
    )
    longest = row_count * seq_count // 4
    hop_count = -(-longest // row_count)
    packets = [from_behind(packet, "seq", k + 1) for k in range(hop_count)]
    (mixed_local,) = call(
        functools.partial(local_kernel, lengths.shape[0], local_heads),
        [((row_count, channels), jnp.float32)],
        [],
        3e9,
        meta,
        bc,
        xc,
        drive,
        cum,
        cum_t,
        lanes(d_skip),
    )
    state_in, placed = call(
        functools.partial(cache_kernel, lengths.shape[0], local_heads),
        [
            ((channels, state_size), jnp.bfloat16),
            ((lengths.shape[0], channels, state_size), jnp.bfloat16),
        ],
        [],
        1e9,
        meta,
        bc,
        drive_wt,
        cum,
        jnp.stack(packets),
    )
    state_cache = (
        lax.psum_scatter(placed, "seq", scatter_dimension=0, tiled=True)
        .astype(jnp.float32)
        .reshape(1, local_heads, head_width, state_size)
    )
    gated, square_part = call(
        functools.partial(gate_kernel, local_heads),
        [((row_count, channels), jnp.bfloat16), ((row_count, LANES), jnp.float32)],
        [],
        1e9,
        mixed_local,
        gate_raw,
        bc,
        state_in,
        lead,
        norm_gain[None],
    )
    mix_term = jnp.dot(gated, out_w, preferred_element_type=jnp.float32)
    square_sum = lax.psum_scatter(square_part[:, 0], "exp", scatter_dimension=0, tiled=True)
    row_scale = lax.rsqrt(square_sum / DI + epsilon)[:, None]
    mixer_out = lax.psum_scatter(
        mix_term.astype(jnp.bfloat16), "exp", scatter_dimension=0, tiled=True
    ).astype(jnp.float32) * row_scale
    residual = tokens.astype(jnp.float32) + mixer_out
    normed = rms_rows(residual, post_gain).astype(jnp.bfloat16)
    normed_all = lax.all_gather(normed, "exp", axis=0, tiled=True)
    shared_hidden = (
        jax.nn.silu(jnp.dot(normed_all, sh_gate, preferred_element_type=jnp.float32))
        * jnp.dot(normed_all, sh_up, preferred_element_type=jnp.float32)
    ).astype(jnp.bfloat16)
    shared = lax.psum_scatter(
        jnp.dot(shared_hidden, sh_down, preferred_element_type=jnp.float32).astype(jnp.bfloat16),
        "exp",
        scatter_dimension=0,
        tiled=True,
    ).astype(jnp.float32)
    top_count = routes.shape[1]
    owned = ex_gate.shape[0]
    experts = owned * seq_count
    capacity = own_rows * top_count * 4 // (3 * experts)
    flat_routes = routes.reshape(-1)
    onehot = (flat_routes[:, None] == jnp.arange(experts, dtype=jnp.int32)[None, :]).astype(
        jnp.int32
    )
    slot_rank = jnp.sum(onehot * (jnp.cumsum(onehot, axis=0) - 1), axis=1)
    slot_idx = flat_routes * capacity + slot_rank
    owner_tok = jnp.arange(own_rows * top_count, dtype=jnp.int32) // top_count
    slot_tok = jnp.full((experts * capacity,), own_rows, jnp.int32).at[slot_idx].set(owner_tok)
    padded = jnp.concatenate([normed, jnp.zeros((1, width), jnp.bfloat16)])
    outgoing = padded[slot_tok].reshape(seq_count, owned, capacity, width)
    received = lax.all_to_all(outgoing, "seq", split_axis=0, concat_axis=0, tiled=True)
    gate_part = jnp.einsum("secd,edf->secf", received, ex_gate, preferred_element_type=jnp.float32)
    up_part = jnp.einsum("secd,edf->secf", received, ex_up, preferred_element_type=jnp.float32)
    hidden = (jax.nn.silu(gate_part) * up_part).astype(jnp.bfloat16)
    expert_out = jnp.einsum(
        "secf,efd->secd", hidden, ex_down, preferred_element_type=jnp.float32
    ).astype(jnp.bfloat16)
    returned = lax.all_to_all(expert_out, "seq", split_axis=0, concat_axis=0, tiled=True)
    picked = returned.reshape(experts * capacity, width)[slot_idx].reshape(
        own_rows, top_count, width
    )
    routed = jnp.sum(gates[:, :, None] * picked.astype(jnp.float32), axis=1)
    layer_out = (residual + shared + routed).astype(jnp.bfloat16)
    return (layer_out, state_cache)


def solution(mesh):
    placed = (
        P(("seq", "exp"), None),
        P(),
        P(None, "exp"),
        P(None, "exp"),
        P(),
        P(None, "exp"),
        P(None, "exp"),
        P(),
        P("exp"),
        P("exp"),
        P("exp"),
        P("exp"),
        P("exp", None),
        P(),
        P(None, "exp"),
        P(None, "exp"),
        P("exp", None),
        P("seq", None, None),
        P("seq", None, None),
        P("seq", None, None),
        P(("seq", "exp"), None),
        P(("seq", "exp"), None),
        P(),
        P(),
    )
    return jax.shard_map(
        body,
        mesh=mesh,
        in_specs=placed,
        out_specs=(P(("seq", "exp"), None), P("seq", "exp", None, None)),
        check_vma=False,
    )
```

```python
import functools
import jax
import jax.numpy as jnp
from jax import lax
from jax.experimental import pallas as pl
from jax.experimental.pallas import tpu as pltpu
from jax.sharding import PartitionSpec as P

DI = 3072


epsilon = 1e-05
highest = lax.Precision.HIGHEST


def from_behind(block, axis, distance):
    devices = range(lax.axis_size(axis))
    route = [(i - distance, i) for i in devices if i - distance in devices]
    return lax.ppermute(block, axis, route)


def rms_rows(values, gain):
    meansq = jnp.mean(values * values, axis=-1, keepdims=True)
    return values * lax.rsqrt(meansq + epsilon) * gain


LANES = 128
HALF = 64


def call(kernel, outs, scratch, flops, *operands):
    moved = sum(v.size * v.dtype.itemsize for v in operands)
    smem = [v.dtype == jnp.int32 and v.ndim == 1 for v in operands]
    return pl.pallas_call(
        kernel,
        out_shape=[jax.ShapeDtypeStruct(s, t) for s, t in outs],
        in_specs=[pl.BlockSpec(memory_space=pltpu.SMEM if m else pltpu.VMEM) for m in smem],
        out_specs=[pl.BlockSpec(memory_space=pltpu.VMEM) for _ in outs],
        scratch_shapes=scratch,
        compiler_params=pltpu.CompilerParams(vmem_limit_bytes=48 * 1024 * 1024),
        cost_estimate=pl.CostEstimate(flops=int(flops), bytes_accessed=moved, transcendentals=0),
    )(*operands)


def positions(shape, axis, start, lag=0):
    return lax.broadcasted_iota(jnp.int32, shape, axis) + (start - lag)


def segments(pos, meta, req_count):
    seg = jnp.zeros(pos.shape, jnp.int32)
    for req in range(req_count):
        seg = seg + (pos >= meta[1 + req]).astype(jnp.int32)
    return seg


def scalar_segment(pos, meta, req_count):
    seg = jnp.int32(0)
    for req in range(req_count):
        seg = seg + (pos >= meta[1 + req]).astype(jnp.int32)
    return seg


def before_segment(meta, req_count):
    start = meta[0]
    return jnp.where(start > 0, scalar_segment(start - 1, meta, req_count), -1)


def by_head(values, pair):
    rows = values.shape[0]
    lane = lax.broadcasted_iota(jnp.int32, (rows, LANES), 1)
    return jnp.where(lane < HALF, values[:, 2 * pair : 2 * pair + 1], values[:, 2 * pair + 1 : 2 * pair + 2])


def front_kernel(
    req_count, heads, meta, xin, bcin, dt_raw, edge, conv_x, conv_bc, dt_bias, a_log,
    xc, bc, drive, drive_wt, cum, cum_t, lead, packet, ext,
):
    rows, channels = xin.shape
    start = meta[0]
    ext[0:8, :] = edge[8:16, :].astype(jnp.float32)
    ext[8:, :channels] = xin[...].astype(jnp.float32)
    ext[8:, channels:] = bcin[...].astype(jnp.float32)
    shape = (rows, LANES)
    seg = segments(positions(shape, 0, start), meta, req_count)
    kept = []
    for lag in (3, 2, 1):
        pos = positions(shape, 0, start, lag)
        kept.append((segments(pos, meta, req_count) == seg) & (pos >= 0))
    kept.append(None)

    def conv(column, weight, offset):
        total = jnp.zeros(shape, jnp.float32)
        for tap in range(4):
            window = ext[5 + tap : 5 + tap + rows, column : column + LANES]
            term = weight[tap : tap + 1, offset : offset + LANES] * window
            total = total + (term if kept[tap] is None else jnp.where(kept[tap], term, 0.0))
        return (total * jax.nn.sigmoid(total)).astype(jnp.bfloat16)

    for part in range(2):
        bc[:, part * LANES : (part + 1) * LANES] = conv(channels + part * LANES, conv_bc, part * LANES)
    raw = dt_raw[...].astype(jnp.float32) + dt_bias[...]
    step = jnp.maximum(raw, 0.0) + jnp.log1p(jnp.exp(-jnp.abs(raw)))
    log_decay = -step * jnp.exp(a_log[...])
    lower = (
        lax.broadcasted_iota(jnp.int32, (rows, rows), 0)
        >= lax.broadcasted_iota(jnp.int32, (rows, rows), 1)
    ).astype(jnp.float32)
    total = jnp.dot(lower, log_decay, precision=highest, preferred_element_type=jnp.float32)
    cum[...] = total
    cum_t[...] = total.T
    seg_before = before_segment(meta, req_count)
    lead[...] = jnp.where(seg == seg_before, jnp.exp(total), 0.0)
    seg_end = total
    for req in range(req_count):
        row = jnp.clip(meta[1 + req] - 1 - start, 0, rows - 1)
        seg_end = jnp.where(seg == req, cum[pl.ds(row, 1), :], seg_end)
    weight = step * jnp.exp(jnp.minimum(seg_end - total, 0.0))
    seg_last = scalar_segment(start + rows - 1, meta, req_count)
    b_last = jnp.where(seg == seg_last, bc[:, :LANES].astype(jnp.float32), 0.0).astype(jnp.bfloat16)
    for pair in range(heads // 2):
        cols = slice(pair * LANES, (pair + 1) * LANES)
        values = conv(pair * LANES, conv_x, pair * LANES)
        xc[:, cols] = values
        wide = values.astype(jnp.float32)
        drive[:, cols] = (wide * by_head(step, pair)).astype(jnp.bfloat16)
        turned = (wide * by_head(weight, pair)).T.astype(jnp.bfloat16)
        drive_wt[cols, :] = turned
        packet[cols, :] = jnp.dot(turned, b_last, preferred_element_type=jnp.float32).astype(jnp.bfloat16)
    passing = jnp.where(seg_last == seg_before, jnp.exp(total[rows - 1 : rows, :]), 0.0)
    high = passing.astype(jnp.bfloat16).astype(jnp.float32)
    row = lax.broadcasted_iota(jnp.int32, (16, LANES), 0)
    packet[channels:, :] = jnp.where(row == 0, high, jnp.where(row == 1, passing - high, 0.0)).astype(jnp.bfloat16)


def local_kernel(req_count, heads, meta, bc, xc, drive, cum, cum_t, d_skip, mixed):
    rows = xc.shape[0]
    start = meta[0]
    tile = LANES
    lane = lax.broadcasted_iota(jnp.int32, (tile, LANES), 1)
    for i in range(rows // tile):
        at = slice(i * tile, (i + 1) * tile)
        width = (i + 1) * tile
        pos_t = positions((tile, width), 0, start + i * tile)
        pos_s = positions((tile, width), 1, start)
        seg_t = segments(positions((tile, LANES), 0, start + i * tile), meta, req_count)[:, 0:1]
        seg_s = segments(positions((8, width), 1, start), meta, req_count)[0:1, :]
        scores = lax.dot_general(
            bc[at, LANES:], bc[0:width, :LANES], (((1,), (1,)), ((), ())), preferred_element_type=jnp.float32
        )
        scores = jnp.where((seg_t == seg_s) & (pos_t >= pos_s), scores, 0.0)
        for pair in range(heads // 2):
            cols = slice(pair * LANES, (pair + 1) * LANES)
            parts = []
            for head in (2 * pair, 2 * pair + 1):
                gap = cum[at, head : head + 1] - cum_t[head : head + 1, 0:width]
                decayed = (scores * jnp.exp(jnp.minimum(gap, 0.0))).astype(jnp.bfloat16)
                parts.append(jnp.dot(decayed, drive[0:width, cols], preferred_element_type=jnp.float32))
            skip = by_head(d_skip[...], pair) * xc[at, cols].astype(jnp.float32)
            mixed[at, cols] = jnp.where(lane < HALF, parts[0], parts[1]) + skip


def cache_kernel(req_count, heads, meta, bc, drive_wt, cum, packets, state_in, placed):
    channels, rows = drive_wt.shape
    start = meta[0]
    hops = packets.shape[0]
    for head in range(heads):
        at = slice(head * HALF, (head + 1) * HALF)
        state = packets[hops - 1, at, :].astype(jnp.float32)
        for hop in range(hops - 2, -1, -1):
            passing = packets[hop, channels : channels + 16, head : head + 1].astype(jnp.float32)
            scale = passing[0:1] + passing[1:2]
            state = scale * state + packets[hop, at, :].astype(jnp.float32)
        state_in[at, :] = state.astype(jnp.bfloat16)
    seg = segments(positions((rows, LANES), 0, start), meta, req_count)
    seg_before = before_segment(meta, req_count)
    for req in range(req_count):
        slot = meta[1 + req_count + req]
        end = meta[1 + req] - 1 - start
        inside = (end >= 0) & (end < rows)

        @pl.when(inside)
        def _():
            b_own = jnp.where(seg == req, bc[:, :LANES].astype(jnp.float32), 0.0).astype(jnp.bfloat16)
            last = cum[pl.ds(jnp.clip(end, 0, rows - 1), 1), :]
            holding = jnp.where(seg_before == req, jnp.exp(last), 0.0)
            fresh = jnp.dot(drive_wt[...], b_own, preferred_element_type=jnp.float32)
            for head in range(heads):
                at = slice(head * HALF, (head + 1) * HALF)
                held = holding[:, head : head + 1] * state_in[at, :].astype(jnp.float32)
                placed[slot, at, :] = (fresh[at] + held).astype(jnp.bfloat16)

        @pl.when(jnp.logical_not(inside))
        def _():
            placed[slot] = jnp.zeros((channels, LANES), jnp.bfloat16)


def gate_kernel(heads, mixed, gate_raw, bc, state_in, lead, gain, out_w, term, gated):
    rows = mixed.shape[0]
    total = jnp.zeros((rows, LANES), jnp.float32)
    for pair in range(heads // 2):
        cols = slice(pair * LANES, (pair + 1) * LANES)
        carried = lax.dot_general(
            bc[:, LANES:], state_in[cols, :], (((1,), (1,)), ((), ())), preferred_element_type=jnp.float32
        )
        raw = gate_raw[:, cols].astype(jnp.float32)
        value = (mixed[:, cols] + by_head(lead[...], pair) * carried) * (raw * jax.nn.sigmoid(raw))
        total = total + value * value
        gated[:, cols] = (value * gain[:, cols]).astype(jnp.bfloat16)
    width = out_w.shape[1]
    for column in range(0, width, 512):
        product = jnp.dot(gated[...], out_w[:, column : column + 512], preferred_element_type=jnp.float32)
        term[:, column : column + 512] = product.astype(jnp.bfloat16)
    square = jnp.sum(total, axis=1, keepdims=True)
    term[:, width:] = jnp.broadcast_to(square, (rows, LANES)).astype(jnp.bfloat16)


def route_kernel(count, capacity, first, routing, dispatch, combine):
    slots = dispatch.shape[1]
    rows = dispatch.shape[2]
    top = routing.shape[1] // 2
    slot = lax.broadcasted_iota(jnp.int32, (rows, slots), 1)
    expert = (first[0] + slot // capacity).astype(jnp.float32)
    place = (slot % capacity).astype(jnp.float32)
    lower = (
        lax.broadcasted_iota(jnp.int32, (rows, rows), 0) >= lax.broadcasted_iota(jnp.int32, (rows, rows), 1)
    ).astype(jnp.bfloat16)
    for source in range(count):
        at = slice(source * rows, (source + 1) * rows)
        named = jnp.zeros((rows, slots), jnp.float32)
        weight = jnp.zeros((rows, slots), jnp.float32)
        for k in range(top):
            hit = routing[at, k : k + 1] == expert
            named = jnp.where(hit, 1.0, named)
            weight = jnp.where(hit, routing[at, top + k : top + k + 1], weight)
        rank = jnp.dot(lower, named.astype(jnp.bfloat16), preferred_element_type=jnp.float32) - 1.0
        chosen = jnp.where(rank == place, named, 0.0)
        dispatch[source] = chosen.T.astype(jnp.bfloat16)
        combine[source] = (chosen * weight).astype(jnp.bfloat16)


def ring_seq(place, count):
    half = place // (count // 2)
    return 2 * place * (1 - half) + (2 * (count - 1 - place) + 1) * half


def ring_place(count):
    me = lax.axis_index("seq")
    column = lax.rem(me, 2)
    depth = me // 2
    return depth * (1 - column) + (count - 1 - depth) * column


def ring_enter(count):
    place = ring_place(count)
    right = ring_seq(lax.rem(place + 1, count), count)
    left = ring_seq(lax.rem(place + count - 1, count), count)
    exp = lax.axis_index("exp")
    barrier = pltpu.get_barrier_semaphore()
    for neighbour in (left, right):
        pl.semaphore_signal(barrier, inc=1, device_id=(neighbour, exp), device_id_type=pl.DeviceIdType.MESH)
    pl.semaphore_wait(barrier, 2)
    return place, (right, exp), (left, exp)


def remote(source, target, send, receive, device):
    return pltpu.make_async_remote_copy(
        src_ref=source,
        dst_ref=target,
        send_sem=send,
        recv_sem=receive,
        device_id=device,
        device_id_type=pl.DeviceIdType.MESH,
    )


def ring_experts_kernel(
    count, normed, dispatch, gate_hbm, up_hbm, down_hbm, result,
    blocks, rows_in, gate_w, up_w, down_w, weight_sem, send_sem, recv_sem,
):
    loads = []
    for i, (source, target) in enumerate(((gate_hbm, gate_w), (up_hbm, up_w), (down_hbm, down_w))):
        loads.append(pltpu.make_async_copy(source, target, weight_sem.at[i]))
        loads[-1].start()
    place, right, left = ring_enter(count)
    own_rows = normed.shape[0]
    owned = gate_w.shape[0]
    capacity = dispatch.shape[1] // owned
    middle = count // 2

    def deal(slot, block):
        source = ring_seq(lax.rem(place + count - slot, count), count)
        picked = jnp.dot(dispatch[source], block[...], preferred_element_type=jnp.float32).astype(jnp.bfloat16)
        for expert in range(owned):
            rows_in[expert, slot * capacity : (slot + 1) * capacity, :] = picked[
                expert * capacity : (expert + 1) * capacity
            ]

    flying = []
    for step in range(1, middle + 1):
        from_left, from_right = step - 1, (count - step + 1) % count
        pair = []
        for way, (held, device) in enumerate(((from_left, right), (from_right, left))):
            source = normed if step == 1 else blocks.at[held]
            if step < middle:
                target = blocks.at[step if way == 0 else count - step]
            else:
                part = pl.ds(way * (own_rows // 2), own_rows // 2)
                source = source.at[part]
                target = blocks.at[middle, part]
            pair.append(remote(source, target, send_sem.at[way, step], recv_sem.at[way, step], device))
            pair[-1].start()
        if step == 1:
            deal(0, normed)
        else:
            deal(step - 1, blocks.at[step - 1])
            deal(count - step + 1, blocks.at[count - step + 1])
        for copy in pair:
            copy.wait_recv()
        flying += pair
    deal(middle, blocks.at[middle])
    for copy in flying:
        copy.wait_send()
    for load in loads:
        load.wait()

    def expert_step(expert, carry):
        rows = rows_in[expert]
        gate = jnp.dot(rows, gate_w[expert], preferred_element_type=jnp.float32)
        up = jnp.dot(rows, up_w[expert], preferred_element_type=jnp.float32)
        hidden = (gate * jax.nn.sigmoid(gate) * up).astype(jnp.bfloat16)
        for column in range(0, result.shape[2], 512):
            out = jnp.dot(hidden, down_w[expert, :, column : column + 512], preferred_element_type=jnp.float32)
            result[expert, :, column : column + 512] = out.astype(jnp.bfloat16)
        return carry

    lax.fori_loop(0, owned, expert_step, 0)


def ring_experts(normed, dispatch, ex_gate, ex_up, ex_down):
    count = dispatch.shape[0]
    owned = ex_gate.shape[0]
    rows = count * dispatch.shape[1] // owned
    own_rows, width = normed.shape
    vmem, far = pl.BlockSpec(memory_space=pltpu.VMEM), pl.BlockSpec(memory_space=pl.ANY)
    return pl.pallas_call(
        functools.partial(ring_experts_kernel, count),
        out_shape=jax.ShapeDtypeStruct((owned, rows, width), jnp.bfloat16),
        in_specs=[vmem, vmem, far, far, far],
        out_specs=vmem,
        scratch_shapes=[
            pltpu.VMEM((count, own_rows, width), jnp.bfloat16),
            pltpu.VMEM((owned, rows, width), jnp.bfloat16),
            pltpu.VMEM(ex_gate.shape, jnp.bfloat16),
            pltpu.VMEM(ex_up.shape, jnp.bfloat16),
            pltpu.VMEM(ex_down.shape, jnp.bfloat16),
            pltpu.SemaphoreType.DMA((3,)),
            pltpu.SemaphoreType.DMA((2, count // 2 + 1)),
            pltpu.SemaphoreType.DMA((2, count // 2 + 1)),
        ],
        compiler_params=pltpu.CompilerParams(
            collective_id=1, has_side_effects=True, vmem_limit_bytes=48 * 1024 * 1024
        ),
        cost_estimate=pl.CostEstimate(flops=40_000_000_000, bytes_accessed=30_000_000, transcendentals=0),
    )(normed, dispatch, ex_gate, ex_up, ex_down)


def ring_sum_kernel(count, outs, combine, tied, total, stage, landed, send_sem, recv_sem):
    place, right, left = ring_enter(count)
    owned, rows, width = outs.shape
    capacity = rows // count
    own_rows = combine.shape[1]
    half, piece_rows = width // 2, own_rows // 2

    def partial(slot, way, piece):
        source = ring_seq(lax.rem(place + count - slot, count), count)
        columns = slice(way * half, (way + 1) * half)
        held = jnp.concatenate(
            [outs[e, slot * capacity : (slot + 1) * capacity, columns] for e in range(owned)], axis=0
        )
        weights = combine[source, piece * piece_rows : (piece + 1) * piece_rows, :]
        return jnp.dot(weights, held, preferred_element_type=jnp.float32)

    flying = {}
    for step in range(count):
        for piece in range(2):
            at = slice(piece * piece_rows, (piece + 1) * piece_rows)
            for way, device in enumerate((right, left)):
                slot = (step + 1) % count if way == 0 else (count - 1 - step) % count
                value = partial(slot, way, piece)
                if step > 0:
                    flying[way, step - 1, piece].wait_recv()
                    value = value + landed[way, step - 1, at, :].astype(jnp.float32)
                if step == count - 1:
                    total[at, way * half : (way + 1) * half] = value
                    continue
                stage[way, step, at, :] = value.astype(jnp.bfloat16)
                copy = remote(
                    stage.at[way, step, pl.ds(piece * piece_rows, piece_rows)],
                    landed.at[way, step, pl.ds(piece * piece_rows, piece_rows)],
                    send_sem.at[way, step, piece],
                    recv_sem.at[way, step, piece],
                    device,
                )
                copy.start()
                flying[way, step, piece] = copy
    for copy in flying.values():
        copy.wait_send()


def ring_sum(outs, combine, tied):
    count, own_rows, _ = combine.shape
    width = outs.shape[2]
    vmem, far = pl.BlockSpec(memory_space=pltpu.VMEM), pl.BlockSpec(memory_space=pl.ANY)
    return pl.pallas_call(
        functools.partial(ring_sum_kernel, count),
        out_shape=jax.ShapeDtypeStruct((own_rows, width), jnp.float32),
        in_specs=[vmem, vmem, far],
        out_specs=vmem,
        scratch_shapes=[
            pltpu.VMEM((2, count - 1, own_rows, width // 2), jnp.bfloat16),
            pltpu.VMEM((2, count - 1, own_rows, width // 2), jnp.bfloat16),
            pltpu.SemaphoreType.DMA((2, count - 1, 2)),
            pltpu.SemaphoreType.DMA((2, count - 1, 2)),
        ],
        compiler_params=pltpu.CompilerParams(
            collective_id=2, has_side_effects=True, vmem_limit_bytes=48 * 1024 * 1024
        ),
        cost_estimate=pl.CostEstimate(flops=40_000_000_000, bytes_accessed=10_000_000, transcendentals=0),
    )(outs, combine, tied)


def body(
    tokens,
    in_gain,
    in_z,
    in_x,
    in_bc,
    in_dt,
    conv_x,
    conv_bc,
    dt_bias,
    a_log,
    d_skip,
    norm_gain,
    out_w,
    post_gain,
    sh_gate,
    sh_up,
    sh_down,
    ex_gate,
    ex_up,
    ex_down,
    routes,
    gates,
    lengths,
    cache_slot,
):
    seq_count = lax.axis_size("seq")
    own_rows = tokens.shape[0]
    width = tokens.shape[1]
    state_size = in_bc.shape[1] // 2
    local_heads = a_log.shape[0]
    head_width = conv_x.shape[1] // local_heads
    stream = lax.all_gather(tokens, "exp", axis=0, tiled=True)
    owned = ex_gate.shape[0]
    capacity = own_rows * routes.shape[1] * 4 // (3 * owned * seq_count)
    packed = jnp.concatenate([routes.astype(jnp.float32), gates], axis=1)
    routing = lax.all_gather(packed, "seq", axis=0, tiled=True)
    first = jnp.reshape(lax.axis_index("seq") * owned, (1,)).astype(jnp.int32)
    dispatch, combine = call(
        functools.partial(route_kernel, seq_count, capacity),
        [
            ((seq_count, owned * capacity, own_rows), jnp.bfloat16),
            ((seq_count, own_rows, owned * capacity), jnp.bfloat16),
        ],
        [],
        1e8,
        first,
        routing,
    )
    row_count = stream.shape[0]
    normed_in = rms_rows(stream.astype(jnp.float32), in_gain).astype(jnp.bfloat16)
    conv_in_x = jnp.dot(normed_in, in_x, preferred_element_type=jnp.float32).astype(jnp.bfloat16)
    conv_in_bc = jnp.dot(normed_in, in_bc, preferred_element_type=jnp.float32).astype(jnp.bfloat16)
    dt_raw = jnp.dot(normed_in, jnp.pad(in_dt, ((0, 0), (0, LANES - local_heads))), preferred_element_type=jnp.float32).astype(jnp.bfloat16)
    tail_rows = jnp.concatenate([conv_in_x[row_count - 16 :], conv_in_bc[row_count - 16 :]], axis=1)
    edge_rows = from_behind(tail_rows, "seq", 1)
    gate_raw = jnp.dot(normed_in, in_z, preferred_element_type=jnp.float32).astype(jnp.bfloat16)
    req_ends = jnp.cumsum(lengths)
    stream_start = lax.axis_index("seq") * row_count
    meta = jnp.concatenate([jnp.reshape(stream_start, (1,)), req_ends, cache_slot]).astype(jnp.int32)
    channels = conv_in_x.shape[1]

    def lanes(values):
        return jnp.pad(values, (0, LANES - values.shape[0]))[None]

    xc, bc, drive, drive_wt, cum, cum_t, lead, packet = call(
        functools.partial(front_kernel, lengths.shape[0], local_heads),
        [
            ((row_count, channels), jnp.bfloat16),
            ((row_count, 2 * state_size), jnp.bfloat16),
            ((row_count, channels), jnp.bfloat16),
            ((channels, row_count), jnp.bfloat16),
            ((row_count, LANES), jnp.float32),
            ((LANES, row_count), jnp.float32),
            ((row_count, LANES), jnp.float32),
            ((channels + 16, state_size), jnp.bfloat16),
        ],
        [pltpu.VMEM((row_count + 8, channels + 2 * state_size), jnp.float32)],
        3e8,
        meta,
        conv_in_x,
        conv_in_bc,
        dt_raw,
        edge_rows,
        conv_x,
        conv_bc,
        lanes(dt_bias),
        lanes(a_log),
    )
    longest = row_count * seq_count // 4
    hop_count = -(-longest // row_count)
    packets = [from_behind(packet, "seq", k + 1) for k in range(hop_count)]
    (mixed_local,) = call(
        functools.partial(local_kernel, lengths.shape[0], local_heads),
        [((row_count, channels), jnp.float32)],
        [],
        3e9,
        meta,
        bc,
        xc,
        drive,
        cum,
        cum_t,
        lanes(d_skip),
    )
    state_in, placed = call(
        functools.partial(cache_kernel, lengths.shape[0], local_heads),
        [
            ((channels, state_size), jnp.bfloat16),
            ((lengths.shape[0], channels, state_size), jnp.bfloat16),
        ],
        [],
        1e9,
        meta,
        bc,
        drive_wt,
        cum,
        jnp.stack(packets),
    )
    state_cache = (
        lax.psum_scatter(placed, "seq", scatter_dimension=0, tiled=True)
        .astype(jnp.float32)
        .reshape(1, local_heads, head_width, state_size)
    )
    (mix_term,) = call(
        functools.partial(gate_kernel, local_heads),
        [((row_count, width + LANES), jnp.bfloat16)],
        [pltpu.VMEM((row_count, channels), jnp.bfloat16)],
        3e9,
        mixed_local,
        gate_raw,
        bc,
        state_in,
        lead,
        norm_gain[None],
        out_w,
    )
    mix_sum = lax.psum_scatter(mix_term, "exp", scatter_dimension=0, tiled=True).astype(jnp.float32)
    row_scale = lax.rsqrt(mix_sum[:, width : width + 1] / DI + epsilon)
    mixer_out = mix_sum[:, :width] * row_scale
    residual = tokens.astype(jnp.float32) + mixer_out
    normed = rms_rows(residual, post_gain).astype(jnp.bfloat16)
    normed_all = lax.all_gather(normed, "exp", axis=0, tiled=True)
    expert_out = ring_experts(normed, dispatch, ex_gate, ex_up, ex_down)
    shared_hidden = (
        jax.nn.silu(jnp.dot(normed_all, sh_gate, preferred_element_type=jnp.float32))
        * jnp.dot(normed_all, sh_up, preferred_element_type=jnp.float32)
    ).astype(jnp.bfloat16)
    shared_term = jnp.dot(shared_hidden, sh_down, preferred_element_type=jnp.float32).astype(jnp.bfloat16)
    shared = lax.psum_scatter(shared_term, "exp", scatter_dimension=0, tiled=True).astype(jnp.float32)
    routed = ring_sum(expert_out, combine, shared_term)
    layer_out = (residual + shared + routed).astype(jnp.bfloat16)
    return (layer_out, state_cache)


def solution(mesh):
    placed = (
        P(("seq", "exp"), None),
        P(),
        P(None, "exp"),
        P(None, "exp"),
        P(),
        P(None, "exp"),
        P(None, "exp"),
        P(),
        P("exp"),
        P("exp"),
        P("exp"),
        P("exp"),
        P("exp", None),
        P(),
        P(None, "exp"),
        P(None, "exp"),
        P("exp", None),
        P("seq", None, None),
        P("seq", None, None),
        P("seq", None, None),
        P(("seq", "exp"), None),
        P(("seq", "exp"), None),
        P(),
        P(),
    )
    return jax.shard_map(
        body,
        mesh=mesh,
        in_specs=placed,
        out_specs=(P(("seq", "exp"), None), P("seq", "exp", None, None)),
        check_vma=False,
    )
```

```python
import functools
import jax
import jax.numpy as jnp
from jax import lax
from jax.experimental import pallas as pl
from jax.experimental.pallas import tpu as pltpu
from jax.sharding import PartitionSpec as P

DI = 3072


epsilon = 1e-05
highest = lax.Precision.HIGHEST


def from_behind(block, axis, distance):
    devices = range(lax.axis_size(axis))
    route = [(i - distance, i) for i in devices if i - distance in devices]
    return lax.ppermute(block, axis, route)


def rms_rows(values, gain):
    meansq = jnp.mean(values * values, axis=-1, keepdims=True)
    return values * lax.rsqrt(meansq + epsilon) * gain


LANES = 128
HALF = 64


def call(kernel, outs, scratch, flops, *operands):
    moved = sum(v.size * v.dtype.itemsize for v in operands)
    smem = [v.dtype == jnp.int32 and v.ndim == 1 for v in operands]
    return pl.pallas_call(
        kernel,
        out_shape=[jax.ShapeDtypeStruct(s, t) for s, t in outs],
        in_specs=[pl.BlockSpec(memory_space=pltpu.SMEM if m else pltpu.VMEM) for m in smem],
        out_specs=[pl.BlockSpec(memory_space=pltpu.VMEM) for _ in outs],
        scratch_shapes=scratch,
        compiler_params=pltpu.CompilerParams(vmem_limit_bytes=48 * 1024 * 1024),
        cost_estimate=pl.CostEstimate(flops=int(flops), bytes_accessed=moved, transcendentals=0),
    )(*operands)


def positions(shape, axis, start, lag=0):
    return lax.broadcasted_iota(jnp.int32, shape, axis) + (start - lag)


def segments(pos, meta, req_count):
    seg = jnp.zeros(pos.shape, jnp.int32)
    for req in range(req_count):
        seg = seg + (pos >= meta[1 + req]).astype(jnp.int32)
    return seg


def scalar_segment(pos, meta, req_count):
    seg = jnp.int32(0)
    for req in range(req_count):
        seg = seg + (pos >= meta[1 + req]).astype(jnp.int32)
    return seg


def before_segment(meta, req_count):
    start = meta[0]
    return jnp.where(start > 0, scalar_segment(start - 1, meta, req_count), -1)


def by_head(values, pair):
    rows = values.shape[0]
    lane = lax.broadcasted_iota(jnp.int32, (rows, LANES), 1)
    return jnp.where(lane < HALF, values[:, 2 * pair : 2 * pair + 1], values[:, 2 * pair + 1 : 2 * pair + 2])


def front_kernel(
    req_count, heads, meta, xin, bcin, dt_raw, edge, conv_x, conv_bc, dt_bias, a_log,
    xc, bc, drive, drive_wt, cum, cum_t, lead, packet, ext,
):
    rows, channels = xin.shape
    start = meta[0]
    ext[0:8, :] = edge[8:16, :].astype(jnp.float32)
    ext[8:, :channels] = xin[...].astype(jnp.float32)
    ext[8:, channels:] = bcin[...].astype(jnp.float32)
    shape = (rows, LANES)
    seg = segments(positions(shape, 0, start), meta, req_count)
    kept = []
    for lag in (3, 2, 1):
        pos = positions(shape, 0, start, lag)
        kept.append((segments(pos, meta, req_count) == seg) & (pos >= 0))
    kept.append(None)

    def conv(column, weight, offset):
        total = jnp.zeros(shape, jnp.float32)
        for tap in range(4):
            window = ext[5 + tap : 5 + tap + rows, column : column + LANES]
            term = weight[tap : tap + 1, offset : offset + LANES] * window
            total = total + (term if kept[tap] is None else jnp.where(kept[tap], term, 0.0))
        return (total * jax.nn.sigmoid(total)).astype(jnp.bfloat16)

    for part in range(2):
        bc[:, part * LANES : (part + 1) * LANES] = conv(channels + part * LANES, conv_bc, part * LANES)
    raw = dt_raw[...].astype(jnp.float32) + dt_bias[...]
    step = jnp.maximum(raw, 0.0) + jnp.log1p(jnp.exp(-jnp.abs(raw)))
    log_decay = -step * jnp.exp(a_log[...])
    lower = (
        lax.broadcasted_iota(jnp.int32, (rows, rows), 0)
        >= lax.broadcasted_iota(jnp.int32, (rows, rows), 1)
    ).astype(jnp.float32)
    total = jnp.dot(lower, log_decay, precision=highest, preferred_element_type=jnp.float32)
    cum[...] = total
    cum_t[...] = total.T
    seg_before = before_segment(meta, req_count)
    lead[...] = jnp.where(seg == seg_before, jnp.exp(total), 0.0)
    seg_end = total
    for req in range(req_count):
        row = jnp.clip(meta[1 + req] - 1 - start, 0, rows - 1)
        seg_end = jnp.where(seg == req, cum[pl.ds(row, 1), :], seg_end)
    weight = step * jnp.exp(jnp.minimum(seg_end - total, 0.0))
    seg_last = scalar_segment(start + rows - 1, meta, req_count)
    b_last = jnp.where(seg == seg_last, bc[:, :LANES].astype(jnp.float32), 0.0).astype(jnp.bfloat16)
    for pair in range(heads // 2):
        cols = slice(pair * LANES, (pair + 1) * LANES)
        values = conv(pair * LANES, conv_x, pair * LANES)
        xc[:, cols] = values
        wide = values.astype(jnp.float32)
        drive[:, cols] = (wide * by_head(step, pair)).astype(jnp.bfloat16)
        turned = (wide * by_head(weight, pair)).T.astype(jnp.bfloat16)
        drive_wt[cols, :] = turned
        packet[cols, :] = jnp.dot(turned, b_last, preferred_element_type=jnp.float32).astype(jnp.bfloat16)
    passing = jnp.where(seg_last == seg_before, jnp.exp(total[rows - 1 : rows, :]), 0.0)
    high = passing.astype(jnp.bfloat16).astype(jnp.float32)
    row = lax.broadcasted_iota(jnp.int32, (16, LANES), 0)
    packet[channels:, :] = jnp.where(row == 0, high, jnp.where(row == 1, passing - high, 0.0)).astype(jnp.bfloat16)


def local_kernel(req_count, heads, meta, bc, xc, drive, cum, cum_t, d_skip, mixed):
    rows = xc.shape[0]
    start = meta[0]
    tile = LANES
    lane = lax.broadcasted_iota(jnp.int32, (tile, LANES), 1)
    for i in range(rows // tile):
        at = slice(i * tile, (i + 1) * tile)
        width = (i + 1) * tile
        pos_t = positions((tile, width), 0, start + i * tile)
        pos_s = positions((tile, width), 1, start)
        seg_t = segments(positions((tile, LANES), 0, start + i * tile), meta, req_count)[:, 0:1]
        seg_s = segments(positions((8, width), 1, start), meta, req_count)[0:1, :]
        scores = lax.dot_general(
            bc[at, LANES:], bc[0:width, :LANES], (((1,), (1,)), ((), ())), preferred_element_type=jnp.float32
        )
        scores = jnp.where((seg_t == seg_s) & (pos_t >= pos_s), scores, 0.0)
        for pair in range(heads // 2):
            cols = slice(pair * LANES, (pair + 1) * LANES)
            parts = []
            for head in (2 * pair, 2 * pair + 1):
                gap = cum[at, head : head + 1] - cum_t[head : head + 1, 0:width]
                decayed = (scores * jnp.exp(jnp.minimum(gap, 0.0))).astype(jnp.bfloat16)
                parts.append(jnp.dot(decayed, drive[0:width, cols], preferred_element_type=jnp.float32))
            skip = by_head(d_skip[...], pair) * xc[at, cols].astype(jnp.float32)
            mixed[at, cols] = jnp.where(lane < HALF, parts[0], parts[1]) + skip


def cache_kernel(req_count, heads, meta, bc, drive_wt, cum, packets, state_in, placed):
    channels, rows = drive_wt.shape
    start = meta[0]
    hops = packets.shape[0]
    for head in range(heads):
        at = slice(head * HALF, (head + 1) * HALF)
        state = packets[hops - 1, at, :].astype(jnp.float32)
        for hop in range(hops - 2, -1, -1):
            passing = packets[hop, channels : channels + 16, head : head + 1].astype(jnp.float32)
            scale = passing[0:1] + passing[1:2]
            state = scale * state + packets[hop, at, :].astype(jnp.float32)
        state_in[at, :] = state.astype(jnp.bfloat16)
    seg = segments(positions((rows, LANES), 0, start), meta, req_count)
    seg_before = before_segment(meta, req_count)
    for req in range(req_count):
        slot = meta[1 + req_count + req]
        end = meta[1 + req] - 1 - start
        inside = (end >= 0) & (end < rows)

        @pl.when(inside)
        def _():
            b_own = jnp.where(seg == req, bc[:, :LANES].astype(jnp.float32), 0.0).astype(jnp.bfloat16)
            last = cum[pl.ds(jnp.clip(end, 0, rows - 1), 1), :]
            holding = jnp.where(seg_before == req, jnp.exp(last), 0.0)
            fresh = jnp.dot(drive_wt[...], b_own, preferred_element_type=jnp.float32)
            for head in range(heads):
                at = slice(head * HALF, (head + 1) * HALF)
                held = holding[:, head : head + 1] * state_in[at, :].astype(jnp.float32)
                placed[slot, at, :] = (fresh[at] + held).astype(jnp.bfloat16)

        @pl.when(jnp.logical_not(inside))
        def _():
            placed[slot] = jnp.zeros((channels, LANES), jnp.bfloat16)


def gate_kernel(heads, mixed, gate_raw, bc, state_in, lead, gain, out_w, term, gated):
    rows = mixed.shape[0]
    total = jnp.zeros((rows, LANES), jnp.float32)
    for pair in range(heads // 2):
        cols = slice(pair * LANES, (pair + 1) * LANES)
        carried = lax.dot_general(
            bc[:, LANES:], state_in[cols, :], (((1,), (1,)), ((), ())), preferred_element_type=jnp.float32
        )
        raw = gate_raw[:, cols].astype(jnp.float32)
        value = (mixed[:, cols] + by_head(lead[...], pair) * carried) * (raw * jax.nn.sigmoid(raw))
        total = total + value * value
        gated[:, cols] = (value * gain[:, cols]).astype(jnp.bfloat16)
    width = out_w.shape[1]
    for column in range(0, width, 512):
        product = jnp.dot(gated[...], out_w[:, column : column + 512], preferred_element_type=jnp.float32)
        term[:, column : column + 512] = product.astype(jnp.bfloat16)
    square = jnp.sum(total, axis=1, keepdims=True)
    term[:, width:] = jnp.broadcast_to(square, (rows, LANES)).astype(jnp.bfloat16)


def exp_partners():
    seq, me = lax.axis_index("seq"), lax.axis_index("exp")
    core = lax.rem(me, 2)
    row = me // 2
    across = (seq, (1 - row) * 2 + core)
    beside = (seq, row * 2 + 1 - core)
    barrier = pltpu.get_barrier_semaphore()
    for device in (across, beside):
        pl.semaphore_signal(barrier, inc=1, device_id=device, device_id_type=pl.DeviceIdType.MESH)
    pl.semaphore_wait(barrier, 2)
    return row, core, across, beside


def gather_kernel(tokens, gain, normed, landed, send_sem, recv_sem):
    row, core, across, beside = exp_partners()
    rows = tokens.shape[0]
    pieces = [pl.ds(p * (rows // 2), rows // 2) for p in range(2)]

    def put(block, at, part):
        values = block.astype(jnp.float32)
        base = pl.multiple_of((at * 2 + part) * (rows // 2), rows // 2)
        normed[pl.ds(base, rows // 2), :] = rms_rows(values, gain[...]).astype(jnp.bfloat16)

    over, side, onward = [], [], []
    for p, piece in enumerate(pieces):
        over.append(remote(tokens.at[piece], landed.at[0, piece], send_sem.at[0, p], recv_sem.at[0, p], across))
        over[-1].start()
    for p, piece in enumerate(pieces):
        side.append(remote(tokens.at[piece], landed.at[1, piece], send_sem.at[1, p], recv_sem.at[1, p], beside))
        side[-1].start()
    for p, piece in enumerate(pieces):
        put(tokens[piece, :], row * 2 + core, p)
    for p, piece in enumerate(pieces):
        side[p].wait_recv()
        put(landed[1, piece, :], row * 2 + 1 - core, p)
    for p, piece in enumerate(pieces):
        over[p].wait_recv()
        onward.append(
            remote(landed.at[0, piece], landed.at[2, piece], send_sem.at[2, p], recv_sem.at[2, p], beside)
        )
        onward[-1].start()
        put(landed[0, piece, :], (1 - row) * 2 + core, p)
    for p, piece in enumerate(pieces):
        onward[p].wait_recv()
        put(landed[2, piece, :], (1 - row) * 2 + 1 - core, p)
    for copy in over + side + onward:
        copy.wait_send()


def remote_params(number):
    return pltpu.CompilerParams(collective_id=number, has_side_effects=True, vmem_limit_bytes=48 * 1024 * 1024)


def gather_normed(tokens, gain):
    rows, width = tokens.shape
    count = lax.axis_size("exp")
    if count != 4:
        stream = lax.all_gather(tokens, "exp", axis=0, tiled=True)
        return rms_rows(stream.astype(jnp.float32), gain).astype(jnp.bfloat16)
    vmem = pl.BlockSpec(memory_space=pltpu.VMEM)
    return pl.pallas_call(
        gather_kernel,
        out_shape=jax.ShapeDtypeStruct((count * rows, width), jnp.bfloat16),
        in_specs=[vmem, vmem],
        out_specs=vmem,
        scratch_shapes=[
            pltpu.VMEM((3, rows, width), jnp.bfloat16),
            pltpu.SemaphoreType.DMA((3, 2)),
            pltpu.SemaphoreType.DMA((3, 2)),
        ],
        compiler_params=remote_params(3),
    )(tokens, gain[None])


def finish_rows(total, tokens, gain):
    width = tokens.shape[1]
    scale = lax.rsqrt(total[:, width : width + 1] / DI + epsilon)
    residual = tokens.astype(jnp.float32) + total[:, :width] * scale
    return residual, rms_rows(residual, gain).astype(jnp.bfloat16)


def sum_kernel(term, tokens, gain, packed, residual, block, beside_in, across_in, stage, send_sem, recv_sem):
    row, core, across, beside = exp_partners()
    rows, width = tokens.shape
    part_rows = rows // 2

    def part_of(owner_row, owner_core, part):
        base = ((owner_row * 2 + owner_core) * 2 + part) * part_rows
        return pl.ds(pl.multiple_of(base, part_rows), part_rows)

    side, over = {}, []
    for far in range(2):
        owner_row = 1 - row if far == 0 else row
        for part in range(2):
            at = pl.ds(part * part_rows, part_rows)
            copy = remote(
                term.at[part_of(owner_row, 1 - core, part)],
                beside_in.at[far, at],
                send_sem.at[far, part],
                recv_sem.at[far, part],
                beside,
            )
            copy.start()
            side[far, part] = copy
    for part in range(2):
        at = pl.ds(part * part_rows, part_rows)
        side[0, part].wait_recv()
        pair = term[part_of(1 - row, core, part), :].astype(jnp.float32) + beside_in[0, at, :].astype(jnp.float32)
        stage[at, :] = pair.astype(jnp.bfloat16)
        over.append(remote(stage.at[at], across_in.at[at], send_sem.at[2, part], recv_sem.at[2, part], across))
        over[-1].start()
    block[:, width:] = packed[...]
    for part in range(2):
        at = pl.ds(part * part_rows, part_rows)
        side[1, part].wait_recv()
        total = term[part_of(row, core, part), :].astype(jnp.float32) + beside_in[1, at, :].astype(jnp.float32)
        over[part].wait_recv()
        total = total + across_in[at, :].astype(jnp.float32)
        kept, normed = finish_rows(total, tokens[at, :], gain[...])
        residual[at, :] = kept
        block[at, :width] = normed
    for copy in list(side.values()) + over:
        copy.wait_send()


def sum_rows(term, tokens, gain, packed):
    rows, width = tokens.shape
    wide = term.shape[1]
    if lax.axis_size("exp") != 4:
        total = lax.psum_scatter(term, "exp", scatter_dimension=0, tiled=True).astype(jnp.float32)
        residual, normed = finish_rows(total, tokens, gain)
        return residual, jnp.concatenate([normed, packed], axis=1)
    vmem = pl.BlockSpec(memory_space=pltpu.VMEM)
    return pl.pallas_call(
        sum_kernel,
        out_shape=[
            jax.ShapeDtypeStruct((rows, width), jnp.float32),
            jax.ShapeDtypeStruct((rows, wide), jnp.bfloat16),
        ],
        in_specs=[vmem] * 4,
        out_specs=[vmem] * 2,
        scratch_shapes=[
            pltpu.VMEM((2, rows, wide), jnp.bfloat16),
            pltpu.VMEM((rows, wide), jnp.bfloat16),
            pltpu.VMEM((rows, wide), jnp.bfloat16),
            pltpu.SemaphoreType.DMA((3, 2)),
            pltpu.SemaphoreType.DMA((3, 2)),
        ],
        compiler_params=remote_params(4),
    )(term, tokens, gain[None], packed)


def ring_seq(place, count):
    half = place // (count // 2)
    return 2 * place * (1 - half) + (2 * (count - 1 - place) + 1) * half


def ring_place(count):
    me = lax.axis_index("seq")
    column = lax.rem(me, 2)
    depth = me // 2
    return depth * (1 - column) + (count - 1 - depth) * column


def ring_enter(count):
    place = ring_place(count)
    right = ring_seq(lax.rem(place + 1, count), count)
    left = ring_seq(lax.rem(place + count - 1, count), count)
    exp = lax.axis_index("exp")
    barrier = pltpu.get_barrier_semaphore()
    for neighbour in (left, right):
        pl.semaphore_signal(barrier, inc=1, device_id=(neighbour, exp), device_id_type=pl.DeviceIdType.MESH)
    pl.semaphore_wait(barrier, 2)
    return place, (right, exp), (left, exp)


def remote(source, target, send, receive, device):
    return pltpu.make_async_remote_copy(
        src_ref=source,
        dst_ref=target,
        send_sem=send,
        recv_sem=receive,
        device_id=device,
        device_id_type=pl.DeviceIdType.MESH,
    )


def ring_experts_kernel(
    count, top, capacity, normed, gate_hbm, up_hbm, down_hbm, result, combine,
    blocks, rows_in, gate_w, up_w, down_w, weight_sem, send_sem, recv_sem,
):
    loads = []
    for i, (source, target) in enumerate(((gate_hbm, gate_w), (up_hbm, up_w), (down_hbm, down_w))):
        loads.append(pltpu.make_async_copy(source, target, weight_sem.at[i]))
        loads[-1].start()
    place, right, left = ring_enter(count)
    own_rows = normed.shape[0]
    owned = gate_w.shape[0]
    width = result.shape[2]
    middle = count // 2
    shape = (own_rows, owned * capacity)
    lane = lax.broadcasted_iota(jnp.int32, shape, 1)
    expert_id = (lax.axis_index("seq") * owned + lane // capacity).astype(jnp.float32)
    rank_id = (lane % capacity).astype(jnp.float32)
    lower = (
        lax.broadcasted_iota(jnp.int32, (own_rows, own_rows), 0)
        >= lax.broadcasted_iota(jnp.int32, (own_rows, own_rows), 1)
    )
    lower = jnp.where(lower, 1.0, 0.0).astype(jnp.bfloat16)

    def deal(slot, block):
        routing = block[:, width:].astype(jnp.float32)
        named = jnp.zeros(shape, jnp.float32)
        weight = jnp.zeros(shape, jnp.float32)
        for k in range(top):
            hit = routing[:, k : k + 1] == expert_id
            named = jnp.where(hit, 1.0, named)
            weight = jnp.where(hit, routing[:, top + k : top + k + 1], weight)
        rank = jnp.dot(lower, named.astype(jnp.bfloat16), preferred_element_type=jnp.float32) - 1.0
        chosen = jnp.where(rank == rank_id, named, 0.0)
        combine[slot] = (chosen * weight).astype(jnp.bfloat16)
        dispatch = chosen.T.astype(jnp.bfloat16)
        picked = jnp.dot(dispatch, block[:, :width], preferred_element_type=jnp.float32).astype(jnp.bfloat16)
        for expert in range(owned):
            rows_in[expert, slot * capacity : (slot + 1) * capacity, :] = picked[
                expert * capacity : (expert + 1) * capacity
            ]

    flying = []
    for step in range(1, middle + 1):
        from_left, from_right = step - 1, (count - step + 1) % count
        pair = []
        for way, (held, device) in enumerate(((from_left, right), (from_right, left))):
            source = normed if step == 1 else blocks.at[held]
            if step < middle:
                target = blocks.at[step if way == 0 else count - step]
            else:
                part = pl.ds(way * (own_rows // 2), own_rows // 2)
                source = source.at[part]
                target = blocks.at[middle, part]
            pair.append(remote(source, target, send_sem.at[way, step], recv_sem.at[way, step], device))
            pair[-1].start()
        if step == 1:
            deal(0, normed)
        else:
            deal(step - 1, blocks.at[step - 1])
            deal(count - step + 1, blocks.at[count - step + 1])
        for copy in pair:
            copy.wait_recv()
        flying += pair
    deal(middle, blocks.at[middle])
    for copy in flying:
        copy.wait_send()
    for load in loads:
        load.wait()

    def expert_step(expert, carry):
        rows = rows_in[expert]
        gate = jnp.dot(rows, gate_w[expert], preferred_element_type=jnp.float32)
        up = jnp.dot(rows, up_w[expert], preferred_element_type=jnp.float32)
        hidden = (gate * jax.nn.sigmoid(gate) * up).astype(jnp.bfloat16)
        for column in range(0, result.shape[2], 512):
            out = jnp.dot(hidden, down_w[expert, :, column : column + 512], preferred_element_type=jnp.float32)
            result[expert, :, column : column + 512] = out.astype(jnp.bfloat16)
        return carry

    lax.fori_loop(0, owned, expert_step, 0)


def ring_experts(block, top, capacity, ex_gate, ex_up, ex_down):
    count = lax.axis_size("seq")
    owned, width = ex_gate.shape[:2]
    rows = count * capacity
    own_rows, wide = block.shape
    vmem, far = pl.BlockSpec(memory_space=pltpu.VMEM), pl.BlockSpec(memory_space=pl.ANY)
    return pl.pallas_call(
        functools.partial(ring_experts_kernel, count, top, capacity),
        out_shape=[
            jax.ShapeDtypeStruct((owned, rows, width), jnp.bfloat16),
            jax.ShapeDtypeStruct((count, own_rows, owned * capacity), jnp.bfloat16),
        ],
        in_specs=[vmem, far, far, far],
        out_specs=[vmem, vmem],
        scratch_shapes=[
            pltpu.VMEM((count, own_rows, wide), jnp.bfloat16),
            pltpu.VMEM((owned, rows, width), jnp.bfloat16),
            pltpu.VMEM(ex_gate.shape, jnp.bfloat16),
            pltpu.VMEM(ex_up.shape, jnp.bfloat16),
            pltpu.VMEM(ex_down.shape, jnp.bfloat16),
            pltpu.SemaphoreType.DMA((3,)),
            pltpu.SemaphoreType.DMA((2, count // 2 + 1)),
            pltpu.SemaphoreType.DMA((2, count // 2 + 1)),
        ],
        compiler_params=pltpu.CompilerParams(
            collective_id=1, has_side_effects=True, vmem_limit_bytes=48 * 1024 * 1024
        ),
        cost_estimate=pl.CostEstimate(flops=40_000_000_000, bytes_accessed=30_000_000, transcendentals=0),
    )(block, ex_gate, ex_up, ex_down)


def ring_sum_kernel(count, outs, combine, tied, total, stage, landed, send_sem, recv_sem):
    place, right, left = ring_enter(count)
    owned, rows, width = outs.shape
    capacity = rows // count
    own_rows = combine.shape[1]
    half, piece_rows = width // 2, own_rows // 2

    def partial(slot, way, piece):
        columns = slice(way * half, (way + 1) * half)
        held = jnp.concatenate(
            [outs[e, slot * capacity : (slot + 1) * capacity, columns] for e in range(owned)], axis=0
        )
        weights = combine[slot, piece * piece_rows : (piece + 1) * piece_rows, :]
        return jnp.dot(weights, held, preferred_element_type=jnp.float32)

    flying = {}
    for step in range(count):
        for piece in range(2):
            at = slice(piece * piece_rows, (piece + 1) * piece_rows)
            for way, device in enumerate((right, left)):
                slot = (step + 1) % count if way == 0 else (count - 1 - step) % count
                value = partial(slot, way, piece)
                if step > 0:
                    flying[way, step - 1, piece].wait_recv()
                    value = value + landed[way, step - 1, at, :].astype(jnp.float32)
                if step == count - 1:
                    total[at, way * half : (way + 1) * half] = value
                    continue
                stage[way, step, at, :] = value.astype(jnp.bfloat16)
                copy = remote(
                    stage.at[way, step, pl.ds(piece * piece_rows, piece_rows)],
                    landed.at[way, step, pl.ds(piece * piece_rows, piece_rows)],
                    send_sem.at[way, step, piece],
                    recv_sem.at[way, step, piece],
                    device,
                )
                copy.start()
                flying[way, step, piece] = copy
    for copy in flying.values():
        copy.wait_send()


def ring_sum(outs, combine, tied):
    count, own_rows, _ = combine.shape
    width = outs.shape[2]
    vmem, far = pl.BlockSpec(memory_space=pltpu.VMEM), pl.BlockSpec(memory_space=pl.ANY)
    return pl.pallas_call(
        functools.partial(ring_sum_kernel, count),
        out_shape=jax.ShapeDtypeStruct((own_rows, width), jnp.float32),
        in_specs=[vmem, vmem, far],
        out_specs=vmem,
        scratch_shapes=[
            pltpu.VMEM((2, count - 1, own_rows, width // 2), jnp.bfloat16),
            pltpu.VMEM((2, count - 1, own_rows, width // 2), jnp.bfloat16),
            pltpu.SemaphoreType.DMA((2, count - 1, 2)),
            pltpu.SemaphoreType.DMA((2, count - 1, 2)),
        ],
        compiler_params=pltpu.CompilerParams(
            collective_id=2, has_side_effects=True, vmem_limit_bytes=48 * 1024 * 1024
        ),
        cost_estimate=pl.CostEstimate(flops=40_000_000_000, bytes_accessed=10_000_000, transcendentals=0),
    )(outs, combine, tied)


def body(
    tokens,
    in_gain,
    in_z,
    in_x,
    in_bc,
    in_dt,
    conv_x,
    conv_bc,
    dt_bias,
    a_log,
    d_skip,
    norm_gain,
    out_w,
    post_gain,
    sh_gate,
    sh_up,
    sh_down,
    ex_gate,
    ex_up,
    ex_down,
    routes,
    gates,
    lengths,
    cache_slot,
):
    seq_count = lax.axis_size("seq")
    own_rows = tokens.shape[0]
    width = tokens.shape[1]
    state_size = in_bc.shape[1] // 2
    local_heads = a_log.shape[0]
    head_width = conv_x.shape[1] // local_heads
    capacity = own_rows * routes.shape[1] * 4 // (3 * ex_gate.shape[0] * seq_count)
    packed = jnp.concatenate([routes.astype(jnp.bfloat16), gates.astype(jnp.bfloat16)], axis=1)
    packed = jnp.pad(packed, ((0, 0), (0, LANES - packed.shape[1])))
    row_count = own_rows * lax.axis_size("exp")
    normed_in = gather_normed(tokens, in_gain)
    conv_in_x = jnp.dot(normed_in, in_x, preferred_element_type=jnp.float32).astype(jnp.bfloat16)
    conv_in_bc = jnp.dot(normed_in, in_bc, preferred_element_type=jnp.float32).astype(jnp.bfloat16)
    dt_raw = jnp.dot(normed_in, jnp.pad(in_dt, ((0, 0), (0, LANES - local_heads))), preferred_element_type=jnp.float32).astype(jnp.bfloat16)
    tail_rows = jnp.concatenate([conv_in_x[row_count - 16 :], conv_in_bc[row_count - 16 :]], axis=1)
    edge_rows = from_behind(tail_rows, "seq", 1)
    gate_raw = jnp.dot(normed_in, in_z, preferred_element_type=jnp.float32).astype(jnp.bfloat16)
    req_ends = jnp.cumsum(lengths)
    stream_start = lax.axis_index("seq") * row_count
    meta = jnp.concatenate([jnp.reshape(stream_start, (1,)), req_ends, cache_slot]).astype(jnp.int32)
    channels = conv_in_x.shape[1]

    def lanes(values):
        return jnp.pad(values, (0, LANES - values.shape[0]))[None]

    xc, bc, drive, drive_wt, cum, cum_t, lead, packet = call(
        functools.partial(front_kernel, lengths.shape[0], local_heads),
        [
            ((row_count, channels), jnp.bfloat16),
            ((row_count, 2 * state_size), jnp.bfloat16),
            ((row_count, channels), jnp.bfloat16),
            ((channels, row_count), jnp.bfloat16),
            ((row_count, LANES), jnp.float32),
            ((LANES, row_count), jnp.float32),
            ((row_count, LANES), jnp.float32),
            ((channels + 16, state_size), jnp.bfloat16),
        ],
        [pltpu.VMEM((row_count + 8, channels + 2 * state_size), jnp.float32)],
        3e8,
        meta,
        conv_in_x,
        conv_in_bc,
        dt_raw,
        edge_rows,
        conv_x,
        conv_bc,
        lanes(dt_bias),
        lanes(a_log),
    )
    longest = row_count * seq_count // 4
    hop_count = -(-longest // row_count)
    packets = [from_behind(packet, "seq", k + 1) for k in range(hop_count)]
    (mixed_local,) = call(
        functools.partial(local_kernel, lengths.shape[0], local_heads),
        [((row_count, channels), jnp.float32)],
        [],
        3e9,
        meta,
        bc,
        xc,
        drive,
        cum,
        cum_t,
        lanes(d_skip),
    )
    state_in, placed = call(
        functools.partial(cache_kernel, lengths.shape[0], local_heads),
        [
            ((channels, state_size), jnp.bfloat16),
            ((lengths.shape[0], channels, state_size), jnp.bfloat16),
        ],
        [],
        1e9,
        meta,
        bc,
        drive_wt,
        cum,
        jnp.stack(packets),
    )
    state_cache = (
        lax.psum_scatter(placed, "seq", scatter_dimension=0, tiled=True)
        .astype(jnp.float32)
        .reshape(1, local_heads, head_width, state_size)
    )
    (mix_term,) = call(
        functools.partial(gate_kernel, local_heads),
        [((row_count, width + LANES), jnp.bfloat16)],
        [pltpu.VMEM((row_count, channels), jnp.bfloat16)],
        3e9,
        mixed_local,
        gate_raw,
        bc,
        state_in,
        lead,
        norm_gain[None],
        out_w,
    )
    residual, block = sum_rows(mix_term, tokens, post_gain, packed)
    normed = block[:, :width]
    normed_all = lax.all_gather(normed, "exp", axis=0, tiled=True)
    expert_out, combine = ring_experts(block, routes.shape[1], capacity, ex_gate, ex_up, ex_down)
    shared_hidden = (
        jax.nn.silu(jnp.dot(normed_all, sh_gate, preferred_element_type=jnp.float32))
        * jnp.dot(normed_all, sh_up, preferred_element_type=jnp.float32)
    ).astype(jnp.bfloat16)
    shared_term = jnp.dot(shared_hidden, sh_down, preferred_element_type=jnp.float32).astype(jnp.bfloat16)
    shared = lax.psum_scatter(shared_term, "exp", scatter_dimension=0, tiled=True).astype(jnp.float32)
    routed = ring_sum(expert_out, combine, shared_term)
    layer_out = (residual + shared + routed).astype(jnp.bfloat16)
    return (layer_out, state_cache)


def solution(mesh):
    placed = (
        P(("seq", "exp"), None),
        P(),
        P(None, "exp"),
        P(None, "exp"),
        P(),
        P(None, "exp"),
        P(None, "exp"),
        P(),
        P("exp"),
        P("exp"),
        P("exp"),
        P("exp"),
        P("exp", None),
        P(),
        P(None, "exp"),
        P(None, "exp"),
        P("exp", None),
        P("seq", None, None),
        P("seq", None, None),
        P("seq", None, None),
        P(("seq", "exp"), None),
        P(("seq", "exp"), None),
        P(),
        P(),
    )
    return jax.shard_map(
        body,
        mesh=mesh,
        in_specs=placed,
        out_specs=(P(("seq", "exp"), None), P("seq", "exp", None, None)),
        check_vma=False,
    )
```
